512 devices in a mesh: row: 32 (over y, x_lo, core), col: 16 (over x_hi, z).
Axes of the slice: x: 4 (x_hi: 2, x_lo: 2; x = x_hi * 2 + x_lo), y: 8, z: 8, core: 2. Of those that a mesh axis runs over, the one named last changes fastest.
Arguments:
- object_slices: bfloat16 [2, 2, 4096, 2048], P(None, None, 'row', 'col'), may hold values from -4.1875 to 4.1875
- probe_modes: float32 [4, 2, 128, 128], replicated, may hold values from -3 to 3
- prop_phase: float32 [128, 128], replicated, may hold values from -3.140625 to 3.140625
- measured: float32 [2048, 128, 128], P(('row', 'col')), may hold values from 0 to 4
- counts: int32 [512], P(('row', 'col')), may hold values from 1 to 4, as said below
- coords: int32 [2048, 2], P(('row', 'col')), may hold values from 0 to 3968, as said below
Outputs:
- object_grad: float32 [2, 2, 4096, 2048], P(None, None, 'row', 'col')
- probe_grad: float32 [32, 4, 2, 128, 128], P('row')
The draws below stay inside these ranges and needn't reach their ends.
Inputs may be any that keep to these rules, and one draw needn't show every extreme that they name: The first counts[d] of device d's 4 slots are live; some device holds 4 live slots in every draw. `coords`: rows d * 4 to (d + 1) * 4 - 1 belong to device d = i * (devices along col) + j: their pixel row lies in [i * 128, (i + 1) * 128), their pixel column in [j * 128, (j + 1) * 128), and every patch of 128 x 128 pixels lies inside the object.
All inputs are finite; a program needn't handle non-finite values.
Results may differ from the reference program's by a relative error of at most 0.024.
The reference program's roundings to bfloat16 on the way count: a program that leaves them out, or rounds other values in their place, can miss the bound.
Values may be sent and summed in bfloat16 or wider, within the bound.
No kernel may reach another device: no remote copies, remote signals or barrier semaphores. Data moves between devices by JAX's collectives and lax.ppermute only.
A program may use at most 64 MiB of HBM per device.

```python
import math
import jax
import jax.numpy as jnp
from jax import lax

PATTERN = 128
MODES = 4
SLICES = 2
TILE_ROWS = 128
TILE_COLS = 128
SLOTS_DEV = 4
ROWS = 4096
COLS = 2048
SLOTS = 2048


def draw_counts(key, part):
    key = jax.random.fold_in(key, 11)
    first, second, third = jax.random.split(key, 3)
    devices = ROWS // TILE_ROWS * (COLS // TILE_COLS)
    picker = jax.random.randint(first, (devices,), 0, 6)
    modest = jax.random.randint(second, (devices,), 1, max(SLOTS_DEV // 2, 1) + 1)
    values = jnp.where(picker == 0, SLOTS_DEV, modest)
    chosen = jax.random.randint(third, (), 0, devices)
    values = jnp.where(jnp.arange(devices) == chosen, SLOTS_DEV, values)
    return values.astype(jnp.int32)


def draw_coords(key, part):
    key = jax.random.fold_in(key, 23)
    first, second = jax.random.split(key, 2)
    cols_dev = COLS // TILE_COLS
    slot_ids = jnp.arange(SLOTS, dtype=jnp.int32)
    device = slot_ids // SLOTS_DEV
    band = device // cols_dev
    column = device % cols_dev
    offset_rows = jax.random.randint(first, (SLOTS,), 0, TILE_ROWS)
    offset_cols = jax.random.randint(second, (SLOTS,), 0, TILE_COLS)
    rows_at = jnp.minimum(band * TILE_ROWS + offset_rows, ROWS - PATTERN)
    cols_at = jnp.minimum(column * TILE_COLS + offset_cols, COLS - PATTERN)
    return jnp.stack([rows_at, cols_at], 1).astype(jnp.int32)


def levels(own_key, dims, pieces, low, largest):
    loudness = 1.0
    for dim, blocks in pieces:
        steps = jax.random.uniform(jax.random.fold_in(jax.random.fold_in(own_key, 6), dim), (blocks,), jnp.float32, low / len(pieces), largest / len(pieces))
        loudness = loudness * jnp.repeat(jnp.exp(steps), dims[dim] // blocks).reshape((-1,) + (1,) * (len(dims) - 1 - dim))
    return loudness


def scatter_about(key, shape, spread, most, cuts=(), held_as=jnp.bfloat16):
    level = levels(key, shape, cuts, -0.22, 0.18) if cuts else 1.0
    entries = jax.random.normal(key, shape, jnp.float32) * spread * level
    return jnp.minimum(jnp.maximum(entries, -most), most).astype(held_as)


def setup_inputs(seed: int = 0) -> dict:
    keys = jax.random.split(jax.random.key(seed), 7)
    return {
        "object_slices": scatter_about(keys[0], (SLICES, 2, ROWS, COLS), 0.7, 4.1875, ((2, 32), (3, 16))),
        "probe_modes": scatter_about(keys[1], (MODES, 2, PATTERN, PATTERN), 0.5, 3.0, (), jnp.float32),
        "prop_phase": jnp.clip(jax.random.uniform(keys[2], (PATTERN, PATTERN), jnp.float32, -3.140625, 3.140625), -3.140625, 3.140625),
        "measured": jnp.clip(4.0 * jax.random.uniform(keys[3], (SLOTS, PATTERN, PATTERN), jnp.float32) ** levels(keys[3], (SLOTS, PATTERN, PATTERN), ((0, 512),), -0.2, 0.2), 0.0, 4.0),
        "counts": draw_counts(jax.random.fold_in(keys[6], 71), 0),
        "coords": draw_coords(jax.random.fold_in(keys[6], 71), 0),
    }


def dft_tables(size):
    steps_idx = jnp.arange(size, dtype=jnp.int32)
    product_idx = steps_idx[:, None] * steps_idx[None, :] % size
    angle = product_idx.astype(jnp.float32) * (2.0 * math.pi / size)
    scale = 1.0 / math.sqrt(size)
    return ((jnp.cos(angle) * scale).astype(jnp.bfloat16), (jnp.sin(angle) * scale).astype(jnp.bfloat16))

def transform(wave_real, wave_imag, orient, cos_table, sin_table):
    batch = wave_real.shape[0]
    size = wave_real.shape[-1]
    stacked = jnp.concatenate([wave_real, wave_imag], 0).astype(jnp.bfloat16).reshape(2 * batch * size, size)
    table = jnp.concatenate([cos_table, sin_table], 1)
    product = jnp.dot(stacked, table, preferred_element_type=jnp.float32).reshape(2, batch, size, 2, size)
    half_real = product[0, :, :, 0] - orient * product[1, :, :, 1]
    half_imag = orient * product[0, :, :, 1] + product[1, :, :, 0]
    halves = jnp.concatenate([half_real, half_imag], 0).astype(jnp.bfloat16)
    tables = jnp.stack([cos_table, sin_table])
    left = jnp.einsum('tjk,bkl->tbjl', tables.astype(jnp.float32), halves.astype(jnp.float32))
    out_real = left[0, :batch] - orient * left[1, batch:]
    out_imag = orient * left[1, :batch] + left[0, batch:]
    return (out_real, out_imag)

def multiply(a_real, a_imag, b_real, b_imag):
    return (a_real * b_real - a_imag * b_imag, a_real * b_imag + a_imag * b_real)

def multiply_conj(a_real, a_imag, b_real, b_imag):
    return (a_real * b_real + a_imag * b_imag, a_imag * b_real - a_real * b_imag)

def position_grads(patch, probe_modes, prop_real, prop_imag, measured_one, cos_table, sin_table):
    layers = patch.shape[0]
    enter_real, enter_imag = (probe_modes[:, 0], probe_modes[:, 1])
    entering = []
    for which_layer in range(layers):
        entering.append((enter_real, enter_imag))
        leave_real, leave_imag = multiply(enter_real, enter_imag, patch[which_layer, 0], patch[which_layer, 1])
        if which_layer < layers - 1:
            freq_real, freq_imag = transform(leave_real, leave_imag, -1.0, cos_table, sin_table)
            freq_real, freq_imag = multiply(freq_real, freq_imag, prop_real, prop_imag)
            enter_real, enter_imag = transform(freq_real, freq_imag, 1.0, cos_table, sin_table)
    far_real, far_imag = transform(leave_real, leave_imag, -1.0, cos_table, sin_table)
    residual = lax.optimization_barrier(jnp.sum(far_real * far_real + far_imag * far_imag, 0)) - measured_one
    back_real, back_imag = transform(residual * far_real, residual * far_imag, 1.0, cos_table, sin_table)
    slice_grads = [None] * layers
    for which_layer in reversed(range(layers)):
        ent_real, ent_imag = entering[which_layer]
        grad_real, grad_imag = multiply_conj(back_real, back_imag, ent_real, ent_imag)
        slice_grads[which_layer] = jnp.stack([lax.optimization_barrier(jnp.sum(grad_real, 0)), lax.optimization_barrier(jnp.sum(grad_imag, 0))])
        to_real, to_imag = multiply_conj(back_real, back_imag, patch[which_layer, 0], patch[which_layer, 1])
        if which_layer > 0:
            freq_real, freq_imag = transform(to_real, to_imag, -1.0, cos_table, sin_table)
            freq_real, freq_imag = multiply_conj(freq_real, freq_imag, prop_real, prop_imag)
            back_real, back_imag = transform(freq_real, freq_imag, 1.0, cos_table, sin_table)
    return (jnp.stack(slice_grads), jnp.stack([to_real, to_imag], 1))

def reference(object_slices, probe_modes, prop_phase, measured, counts, coords):
    whole = object_slices.astype(jnp.float32)
    cos_table, sin_table = dft_tables(PATTERN)
    prop_real = jnp.cos(prop_phase)
    prop_imag = jnp.sin(prop_phase)
    zero_idx = jnp.zeros((), jnp.int32)
    bands = ROWS // TILE_ROWS
    cols_dev = COLS // TILE_COLS
    region_slots = SLOTS_DEV * cols_dev

    def visit(slot, carry):
        live = slot % SLOTS_DEV < counts[slot // SLOTS_DEV]
        row_at = coords[slot, 0].astype(jnp.int32)
        col_at = coords[slot, 1].astype(jnp.int32)
        starts = (zero_idx, zero_idx, row_at, col_at)
        region = (slot // region_slots).astype(jnp.int32)
        probe_starts = (region, zero_idx, zero_idx, zero_idx, zero_idx)

        def active(state):
            object_acc, probe_acc = state
            patch = lax.dynamic_slice(whole, starts, (SLICES, 2, PATTERN, PATTERN))
            grads, probe_part = position_grads(patch, probe_modes, prop_real, prop_imag, measured[slot], cos_table, sin_table)
            current = lax.dynamic_slice(object_acc, starts, (SLICES, 2, PATTERN, PATTERN))
            object_acc = lax.dynamic_update_slice(object_acc, current + grads, starts)
            held = lax.dynamic_slice(probe_acc, probe_starts, (1, MODES, 2, PATTERN, PATTERN))
            probe_acc = lax.dynamic_update_slice(probe_acc, held + probe_part[None], probe_starts)
            return (object_acc, probe_acc)

        def spare_state(state):
            return state
        return lax.cond(live, active, spare_state, carry)
    init = (jnp.zeros(whole.shape, jnp.float32), jnp.zeros((bands,) + probe_modes.shape, jnp.float32))
    object_grad, probe_acc = lax.fori_loop(0, SLOTS, visit, init)
    return (object_grad, probe_acc * (1.0 / math.sqrt(region_slots)))
```

```python
import math

import jax
import jax.numpy as jnp
from jax import lax
from jax.sharding import PartitionSpec as P


def from_behind(block, axis, distance):
    devices = range(lax.axis_size(axis))
    route = [(i - distance, i) for i in devices if i - distance in devices]
    return lax.ppermute(block, axis, route)


def dft_tables(size):
    steps_idx = jnp.arange(size, dtype=jnp.int32)
    product_idx = steps_idx[:, None] * steps_idx[None, :] % size
    angle = product_idx.astype(jnp.float32) * (2.0 * math.pi / size)
    scale = 1.0 / math.sqrt(size)
    return (
        (jnp.cos(angle) * scale).astype(jnp.bfloat16),
        (jnp.sin(angle) * scale).astype(jnp.bfloat16),
    )


def transform(wave_real, wave_imag, orient, cos_table, sin_table):
    batch = wave_real.shape[0]
    size = wave_real.shape[-1]
    stacked = (
        jnp.concatenate([wave_real, wave_imag], 0)
        .astype(jnp.bfloat16)
        .reshape(2 * batch * size, size)
    )
    table = jnp.concatenate([cos_table, sin_table], 1)
    product = jnp.dot(stacked, table, preferred_element_type=jnp.float32).reshape(
        2, batch, size, 2, size
    )
    half_real = product[0, :, :, 0] - orient * product[1, :, :, 1]
    half_imag = orient * product[0, :, :, 1] + product[1, :, :, 0]
    halves = jnp.concatenate([half_real, half_imag], 0).astype(jnp.bfloat16)
    tables = jnp.stack([cos_table, sin_table])
    left = jnp.einsum("tjk,bkl->tbjl", tables, halves, preferred_element_type=jnp.float32)
    out_real = left[0, :batch] - orient * left[1, batch:]
    out_imag = orient * left[1, :batch] + left[0, batch:]
    return (out_real, out_imag)


def multiply(a_real, a_imag, b_real, b_imag):
    return (a_real * b_real - a_imag * b_imag, a_real * b_imag + a_imag * b_real)


def multiply_conj(a_real, a_imag, b_real, b_imag):
    return (a_real * b_real + a_imag * b_imag, a_imag * b_real - a_real * b_imag)


def position_grads(patch, probe_modes, prop_real, prop_imag, measured_one, cos_table, sin_table):
    layers = patch.shape[0]
    enter_real, enter_imag = (probe_modes[:, 0], probe_modes[:, 1])
    entering = []
    for which_layer in range(layers):
        entering.append((enter_real, enter_imag))
        leave_real, leave_imag = multiply(
            enter_real, enter_imag, patch[which_layer, 0], patch[which_layer, 1]
        )
        if which_layer < layers - 1:
            freq_real, freq_imag = transform(leave_real, leave_imag, -1.0, cos_table, sin_table)
            freq_real, freq_imag = multiply(freq_real, freq_imag, prop_real, prop_imag)
            enter_real, enter_imag = transform(freq_real, freq_imag, 1.0, cos_table, sin_table)
    far_real, far_imag = transform(leave_real, leave_imag, -1.0, cos_table, sin_table)
    residual = jnp.sum(far_real * far_real + far_imag * far_imag, 0) - measured_one
    back_real, back_imag = transform(
        residual * far_real, residual * far_imag, 1.0, cos_table, sin_table
    )
    slice_grads = [None] * layers
    for which_layer in reversed(range(layers)):
        ent_real, ent_imag = entering[which_layer]
        grad_real, grad_imag = multiply_conj(back_real, back_imag, ent_real, ent_imag)
        slice_grads[which_layer] = jnp.stack([jnp.sum(grad_real, 0), jnp.sum(grad_imag, 0)])
        to_real, to_imag = multiply_conj(
            back_real, back_imag, patch[which_layer, 0], patch[which_layer, 1]
        )
        if which_layer > 0:
            freq_real, freq_imag = transform(to_real, to_imag, -1.0, cos_table, sin_table)
            freq_real, freq_imag = multiply_conj(freq_real, freq_imag, prop_real, prop_imag)
            back_real, back_imag = transform(freq_real, freq_imag, 1.0, cos_table, sin_table)
    return (jnp.stack(slice_grads), jnp.stack([to_real, to_imag], 1))


def body(object_slices, probe_modes, prop_phase, measured, counts, coords):
    size = probe_modes.shape[-1]
    layers = object_slices.shape[0]
    tile_rows = object_slices.shape[2]
    tile_cols = object_slices.shape[3]
    col_count = lax.axis_size("col")
    row_index = lax.axis_index("row")
    col_index = lax.axis_index("col")
    lower = from_behind(object_slices, "row", -1)
    taller = jnp.concatenate([object_slices, lower], 2)
    side = from_behind(taller, "col", -1)
    extended = jnp.concatenate([taller, side], 3)
    cos_table, sin_table = dft_tables(size)
    prop_real = jnp.cos(prop_phase)
    prop_imag = jnp.sin(prop_phase)
    zero_idx = jnp.zeros((), jnp.int32)
    start_row = row_index * tile_rows
    start_col = col_index * tile_cols

    def visit(slot, carry):
        ext_grad, probe_acc = carry
        local_row = coords[slot, 0] - start_row
        local_col = coords[slot, 1] - start_col
        starts = (zero_idx, zero_idx, local_row, local_col)
        patch = lax.dynamic_slice(extended, starts, (layers, 2, size, size)).astype(jnp.float32)
        grads, probe_part = position_grads(
            patch, probe_modes, prop_real, prop_imag, measured[slot], cos_table, sin_table
        )
        current = lax.dynamic_slice(ext_grad, starts, (layers, 2, size, size))
        ext_grad = lax.dynamic_update_slice(ext_grad, current + grads, starts)
        return (ext_grad, probe_acc + probe_part)

    init = (jnp.zeros(extended.shape, jnp.float32), jnp.zeros(probe_modes.shape, jnp.float32))
    ext_grad, probe_acc = lax.fori_loop(0, counts[0], visit, init)
    side_back = from_behind(ext_grad[:, :, :, tile_cols:].astype(jnp.bfloat16), "col", 1).astype(
        jnp.float32
    )
    ext_grad = ext_grad.at[:, :, :, :size].add(side_back)
    lower_back = from_behind(
        ext_grad[:, :, tile_rows:, :tile_cols].astype(jnp.bfloat16), "row", 1
    ).astype(jnp.float32)
    owned = ext_grad[:, :, :tile_rows, :tile_cols].at[:, :, :size, :].add(lower_back)
    region_slots = measured.shape[0] * col_count
    shares = probe_acc.astype(jnp.bfloat16).reshape(col_count, -1, probe_acc.shape[-1])
    received = lax.all_to_all(shares, "col", 0, 0, tiled=True)
    share = jnp.sum(received.astype(jnp.float32), 0).astype(jnp.bfloat16)
    spread = lax.all_to_all(
        jnp.broadcast_to(share[None], shares.shape), "col", 0, 0, tiled=True
    )
    probe_total = spread.reshape(probe_acc.shape).astype(jnp.float32)
    return (owned, (probe_total * (1.0 / math.sqrt(region_slots)))[None])


def solution(mesh):
    return jax.shard_map(
        body,
        mesh=mesh,
        in_specs=(
            P(None, None, "row", "col"),
            P(),
            P(),
            P(("row", "col"), None, None),
            P(("row", "col")),
            P(("row", "col"), None),
        ),
        out_specs=(P(None, None, "row", "col"), P("row", None, None, None, None)),
        check_vma=False,
    )
```

```python
import functools
import math

import jax
import jax.numpy as jnp
from jax import lax
from jax.experimental import pallas as pl
from jax.experimental.pallas import tpu as pltpu
from jax.sharding import PartitionSpec as P

GROUP = 2


def from_behind(block, axis, distance):
    devices = range(lax.axis_size(axis))
    route = [(i - distance, i) for i in devices if i - distance in devices]
    return lax.ppermute(block, axis, route)


def dft_matrices(size):
    steps_idx = jnp.arange(size, dtype=jnp.int32)
    product_idx = steps_idx[:, None] * steps_idx[None, :] % size
    angle = product_idx.astype(jnp.float32) * (2.0 * math.pi / size)
    scale = 1.0 / math.sqrt(size)
    cos_table = (jnp.cos(angle) * scale).astype(jnp.bfloat16)
    sin_table = (jnp.sin(angle) * scale).astype(jnp.bfloat16)
    minus = jnp.concatenate(
        [
            jnp.concatenate([cos_table, -sin_table], 1),
            jnp.concatenate([sin_table, cos_table], 1),
        ],
        0,
    )
    plus = jnp.concatenate(
        [
            jnp.concatenate([cos_table, sin_table], 1),
            jnp.concatenate([-sin_table, cos_table], 1),
        ],
        0,
    )
    return jnp.stack([minus, plus])


def swap_blocks(matrix, size):
    upper = jnp.concatenate([matrix[:size, :size], matrix[size:, :size]], 1)
    lower = jnp.concatenate([matrix[:size, size:], matrix[size:, size:]], 1)
    return jnp.concatenate([upper, lower], 0)


def transform(real, imag, first, second):
    size = real.shape[0]
    stacked = jnp.concatenate([real, imag], 0).astype(jnp.bfloat16)
    half = jnp.dot(
        swap_blocks(stacked, size), first, preferred_element_type=jnp.float32
    ).astype(jnp.bfloat16)
    out = jnp.dot(second, swap_blocks(half, size), preferred_element_type=jnp.float32)
    return out[:size], out[size:]


def multiply(a_real, a_imag, b_real, b_imag):
    return (a_real * b_real - a_imag * b_imag, a_real * b_imag + a_imag * b_real)


def multiply_conj(a_real, a_imag, b_real, b_imag):
    return (a_real * b_real + a_imag * b_imag, a_imag * b_real - a_real * b_imag)


def grads_kernel(
    counts_ref,
    corner_ref,
    own_ref,
    right_ref,
    lower_ref,
    probe_ref,
    prop_ref,
    measured_ref,
    dft_ref,
    grad_ref,
    side_ref,
    foot_ref,
    probe_out_ref,
    ext_ref,
    acc_ref,
    enter_ref,
    probe_acc_ref,
):
    size = probe_ref.shape[-1]
    layers = ext_ref.shape[1]
    pairs = probe_ref.shape[0] // 2
    f32, bf16 = jnp.float32, jnp.bfloat16
    ext_ref[0, :, :, :size] = own_ref[...].astype(f32)
    ext_ref[1, :, :, :size] = right_ref[...].astype(f32)
    ext_ref[0, :, :, size:] = lower_ref[0].astype(f32)
    ext_ref[1, :, :, size:] = lower_ref[1].astype(f32)
    acc_ref[...] = jnp.zeros_like(acc_ref)
    probe_acc_ref[...] = jnp.zeros_like(probe_acc_ref)
    for pair in range(pairs):
        for part in range(2):
            enter_ref[pair, part] = jnp.concatenate(
                [probe_ref[2 * pair, part], probe_ref[2 * pair + 1, part]], 1
            )
    minus, plus = dft_ref[0], dft_ref[1]
    forward = functools.partial(transform, first=minus, second=plus)
    inverse = functools.partial(transform, first=plus, second=minus)

    def twice(block):
        return jnp.concatenate([block, block], 1)

    def fold(block):
        return block[:, :size] + block[:, size:]

    def visit(slot, live):
        row, col = corner_ref[slot, 0], corner_ref[slot, 1]
        patch = [
            [
                twice(
                    pltpu.roll(
                        jnp.concatenate(
                            [ext_ref[side, layer, part, pl.ds(row, size), :] for side in range(2)],
                            1,
                        ),
                        lax.rem(2 * size - col, 2 * size),
                        1,
                    )[:, :size]
                )
                for part in range(2)
            ]
            for layer in range(layers)
        ]
        prop = [twice(prop_ref[part]) for part in range(2)]
        entering = [[(enter_ref[pair, 0], enter_ref[pair, 1]) for pair in range(pairs)]]
        far = [None] * pairs
        for layer in range(layers):
            following = []
            for pair in range(pairs):
                leave = multiply(*entering[layer][pair], *patch[layer])
                freq = forward(*leave)
                if layer < layers - 1:
                    following.append(inverse(*multiply(*freq, *prop)))
                else:
                    far[pair] = freq
            entering.append(following)
        power = sum(real * real + imag * imag for real, imag in far)
        residual = jnp.where(live, fold(power) - measured_ref[slot], 0.0)
        residual = twice(residual)
        back = [inverse(residual * real, residual * imag) for real, imag in far]
        slice_grads = [None] * layers
        to_enter = [None] * pairs
        for layer in reversed(range(layers)):
            terms = [multiply_conj(*back[pair], *entering[layer][pair]) for pair in range(pairs)]
            slice_grads[layer] = [fold(sum(term[part] for term in terms)) for part in range(2)]
            for pair in range(pairs):
                to_enter[pair] = multiply_conj(*back[pair], *patch[layer])
                if layer > 0:
                    freq = forward(*to_enter[pair])
                    back[pair] = inverse(*multiply_conj(*freq, *prop))
        return row, col, slice_grads, to_enter

    def visit_group(group, carry):
        done = []
        for which in range(GROUP):
            slot = group * GROUP + which
            done.append(visit(slot, slot < counts_ref[0]))
        for row, col, slice_grads, _ in done:
            for layer in range(layers):
                for part in range(2):
                    block = slice_grads[layer][part]
                    wide = jnp.concatenate([block, jnp.zeros_like(block)], 1)
                    wide = pltpu.roll(wide, col, 1)
                    rows = pl.ds(row, size)
                    acc_ref[0, layer, part, rows, :] += wide[:, :size]
                    acc_ref[1, layer, part, rows, :] += wide[:, size:]
        for pair in range(pairs):
            for part in range(2):
                probe_acc_ref[pair, part] += sum(entry[3][pair][part] for entry in done)
        return carry

    lax.fori_loop(0, (counts_ref[0] + GROUP - 1) // GROUP, visit_group, 0)
    grad_ref[...] = acc_ref[0, :, :, :size]
    side_ref[0] = acc_ref[1, :, :, :size].astype(bf16)
    side_ref[1] = acc_ref[1, :, :, size:].astype(bf16)
    foot_ref[...] = acc_ref[0, :, :, size:]
    for pair in range(pairs):
        for part in range(2):
            both = probe_acc_ref[pair, part].astype(bf16)
            probe_out_ref[2 * pair, part] = both[:, :size]
            probe_out_ref[2 * pair + 1, part] = both[:, size:]


def local_grads(own, right, lower, probe_modes, prop, measured, dft, counts, corners):
    layers, parts, size, _ = own.shape
    modes = probe_modes.shape[0]
    f32, bf16 = jnp.float32, jnp.bfloat16
    vmem = pl.BlockSpec(memory_space=pltpu.VMEM)
    smem = pl.BlockSpec(memory_space=pltpu.SMEM)
    tile = (layers, parts, size, size)
    return pl.pallas_call(
        grads_kernel,
        out_shape=(
            jax.ShapeDtypeStruct(tile, f32),
            jax.ShapeDtypeStruct((2,) + tile, bf16),
            jax.ShapeDtypeStruct(tile, f32),
            jax.ShapeDtypeStruct(probe_modes.shape, bf16),
        ),
        in_specs=[smem] * 2 + [vmem] * 7,
        out_specs=(vmem,) * 4,
        scratch_shapes=[
            pltpu.VMEM((2, layers, parts, 2 * size, size), f32),
            pltpu.VMEM((2, layers, parts, 2 * size, size), f32),
            pltpu.VMEM((modes // 2, 2, size, 2 * size), f32),
            pltpu.VMEM((modes // 2, 2, size, 2 * size), f32),
        ],
        compiler_params=pltpu.CompilerParams(vmem_limit_bytes=40 * 1024 * 1024),
    )(counts, corners, own, right, lower, probe_modes, prop, measured, dft)


def body(object_slices, probe_modes, prop_phase, measured, counts, coords):
    tile_rows = object_slices.shape[2]
    tile_cols = object_slices.shape[3]
    col_count = lax.axis_size("col")
    origin = jnp.stack([lax.axis_index("row") * tile_rows, lax.axis_index("col") * tile_cols])
    corners = coords - origin.astype(jnp.int32)
    dft = dft_matrices(probe_modes.shape[-1])
    prop = jnp.stack([jnp.cos(prop_phase), jnp.sin(prop_phase)])
    right = from_behind(object_slices, "col", -1)
    lower = from_behind(jnp.stack([object_slices, right]), "row", -1)
    grad, side, foot, probe_part = local_grads(
        object_slices, right, lower, probe_modes, prop, measured, dft, counts, corners
    )
    side_back = from_behind(side, "col", 1).astype(jnp.float32)
    shares = probe_part.reshape(col_count, -1, probe_part.shape[-1])
    received = lax.all_to_all(shares, "col", 0, 0, tiled=True)
    foot_back = from_behind((foot + side_back[1]).astype(jnp.bfloat16), "row", 1)
    share = jnp.sum(received.astype(jnp.float32), 0).astype(jnp.bfloat16)
    spread = lax.all_to_all(
        jnp.broadcast_to(share[None], shares.shape), "col", 0, 0, tiled=True
    )
    owned = grad + side_back[0] + foot_back.astype(jnp.float32)
    region_slots = measured.shape[0] * col_count
    probe_total = spread.reshape(probe_part.shape).astype(jnp.float32)
    return (owned, (probe_total * (1.0 / math.sqrt(region_slots)))[None])


def solution(mesh):
    return jax.shard_map(
        body,
        mesh=mesh,
        in_specs=(
            P(None, None, "row", "col"),
            P(),
            P(),
            P(("row", "col"), None, None),
            P(("row", "col")),
            P(("row", "col"), None),
        ),
        out_specs=(P(None, None, "row", "col"), P("row", None, None, None, None)),
        check_vma=False,
    )
```

```python
import functools
import math

import jax
import jax.numpy as jnp
from jax import lax
from jax.experimental import pallas as pl
from jax.experimental.pallas import tpu as pltpu
from jax.sharding import PartitionSpec as P


def from_behind(block, axis, distance):
    devices = range(lax.axis_size(axis))
    route = [(i - distance, i) for i in devices if i - distance in devices]
    return lax.ppermute(block, axis, route)


def dft_matrices(size):
    steps_idx = jnp.arange(size, dtype=jnp.int32)
    product_idx = steps_idx[:, None] * steps_idx[None, :] % size
    angle = product_idx.astype(jnp.float32) * (2.0 * math.pi / size)
    scale = 1.0 / math.sqrt(size)
    cos_table = (jnp.cos(angle) * scale).astype(jnp.bfloat16)
    sin_table = (jnp.sin(angle) * scale).astype(jnp.bfloat16)
    minus = jnp.concatenate(
        [
            jnp.concatenate([cos_table, -sin_table], 1),
            jnp.concatenate([sin_table, cos_table], 1),
        ],
        0,
    )
    plus = jnp.concatenate(
        [
            jnp.concatenate([cos_table, sin_table], 1),
            jnp.concatenate([-sin_table, cos_table], 1),
        ],
        0,
    )
    return jnp.stack([minus, plus])


def swap_blocks(matrix, size):
    upper = jnp.concatenate([matrix[:size, :size], matrix[size:, :size]], 1)
    lower = jnp.concatenate([matrix[:size, size:], matrix[size:, size:]], 1)
    return jnp.concatenate([upper, lower], 0)


def transform(waves, first, second):
    size = waves[0][0].shape[0]
    stacked = [
        swap_blocks(jnp.concatenate([real, imag], 0).astype(jnp.bfloat16), size)
        for real, imag in waves
    ]
    halves = first_stage(stacked, first)
    outs = second_stage([swap_blocks(half, size) for half in halves], second)
    return [(out[:size], out[size:]) for out in outs]


def first_stage(stacked, first):
    rows = stacked[0].shape[0]
    half = jnp.dot(
        jnp.concatenate(stacked, 0), first, preferred_element_type=jnp.float32
    ).astype(jnp.bfloat16)
    return [half[i * rows : (i + 1) * rows] for i in range(len(stacked))]


def second_stage(halves, second):
    cols = halves[0].shape[1]
    out = jnp.dot(second, jnp.concatenate(halves, 1), preferred_element_type=jnp.float32)
    return [out[:, i * cols : (i + 1) * cols] for i in range(len(halves))]


def multiply(a_real, a_imag, b_real, b_imag):
    return (a_real * b_real - a_imag * b_imag, a_real * b_imag + a_imag * b_real)


def multiply_conj(a_real, a_imag, b_real, b_imag):
    return (a_real * b_real + a_imag * b_imag, a_imag * b_real - a_real * b_imag)


def grads_kernel(
    counts_ref,
    corner_ref,
    own_ref,
    right_ref,
    lower_ref,
    probe_ref,
    prop_ref,
    measured_ref,
    dft_ref,
    grad_ref,
    side_ref,
    foot_ref,
    probe_out_ref,
    ext_ref,
    acc_ref,
):
    size = probe_ref.shape[-1]
    layers = ext_ref.shape[1]
    pairs = probe_ref.shape[0] // 2
    f32, bf16 = jnp.float32, jnp.bfloat16
    ext_ref[0, :, :, :size] = own_ref[...].astype(f32)
    ext_ref[1, :, :, :size] = right_ref[...].astype(f32)
    ext_ref[0, :, :, size:] = lower_ref[0].astype(f32)
    ext_ref[1, :, :, size:] = lower_ref[1].astype(f32)
    acc_ref[...] = jnp.zeros_like(acc_ref)
    minus, plus = dft_ref[0], dft_ref[1]
    forward = functools.partial(transform, first=minus, second=plus)
    inverse = functools.partial(transform, first=plus, second=minus)

    def twice(block):
        return jnp.concatenate([block, block], 1)

    def fold(block):
        return block[:, :size] + block[:, size:]

    def load_patch(row, col, layer, part):
        rows = pl.ds(row, size)
        both = jnp.concatenate([ext_ref[side, layer, part, rows, :] for side in range(2)], 1)
        return twice(pltpu.roll(both, lax.rem(2 * size - col, 2 * size), 1)[:, :size])

    slots = range(measured_ref.shape[0])
    corners = [(corner_ref[slot, 0], corner_ref[slot, 1]) for slot in slots]
    patches = [
        [[load_patch(row, col, layer, part) for part in range(2)] for layer in range(layers)]
        for row, col in corners
    ]
    units = [(which, pair) for which in slots for pair in range(pairs)]
    prop = [twice(prop_ref[part]) for part in range(2)]
    probe = [
        tuple(
            jnp.concatenate([probe_ref[2 * pair, part], probe_ref[2 * pair + 1, part]], 1)
            for part in range(2)
        )
        for pair in range(pairs)
    ]
    entering = [[probe[pair] for _, pair in units]]
    for layer in range(layers):
        leaving = [
            multiply(*wave, *patches[which][layer])
            for wave, (which, _) in zip(entering[layer], units)
        ]
        freqs = forward(leaving)
        if layer < layers - 1:
            entering.append(inverse([multiply(*freq, *prop) for freq in freqs]))
    far = freqs
    residuals = []
    for which, slot in enumerate(slots):
        power = sum(
            real * real + imag * imag
            for (real, imag), unit in zip(far, units)
            if unit[0] == which
        )
        residual = jnp.where(slot < counts_ref[0], fold(power) - measured_ref[slot], 0.0)
        residuals.append(twice(residual))
    back = inverse(
        [
            (residuals[which] * real, residuals[which] * imag)
            for (real, imag), (which, _) in zip(far, units)
        ]
    )
    for layer in reversed(range(layers)):
        terms = [
            multiply_conj(*wave, *entered) for wave, entered in zip(back, entering[layer])
        ]
        for which, (row, col) in enumerate(corners):
            for part in range(2):
                block = fold(
                    sum(term[part] for term, unit in zip(terms, units) if unit[0] == which)
                )
                wide = jnp.concatenate([block, jnp.zeros_like(block)], 1)
                wide = pltpu.roll(wide, col, 1)
                rows = pl.ds(row, size)
                acc_ref[0, layer, part, rows, :] += wide[:, :size]
                acc_ref[1, layer, part, rows, :] += wide[:, size:]
        to_enter = [
            multiply_conj(*wave, *patches[which][layer])
            for wave, (which, _) in zip(back, units)
        ]
        if layer > 0:
            back = inverse([multiply_conj(*freq, *prop) for freq in forward(to_enter)])
    for pair in range(pairs):
        for part in range(2):
            both = sum(wave[part] for wave, unit in zip(to_enter, units) if unit[1] == pair)
            both = both.astype(bf16)
            probe_out_ref[2 * pair, part] = both[:, :size]
            probe_out_ref[2 * pair + 1, part] = both[:, size:]
    grad_ref[...] = acc_ref[0, :, :, :size]
    side_ref[0] = acc_ref[1, :, :, :size].astype(bf16)
    side_ref[1] = acc_ref[1, :, :, size:].astype(bf16)
    foot_ref[...] = acc_ref[0, :, :, size:]


def local_grads(own, right, lower, probe_modes, prop, measured, dft, counts, corners):
    layers, parts, size, _ = own.shape
    f32, bf16 = jnp.float32, jnp.bfloat16
    vmem = pl.BlockSpec(memory_space=pltpu.VMEM)
    smem = pl.BlockSpec(memory_space=pltpu.SMEM)
    tile = (layers, parts, size, size)
    return pl.pallas_call(
        grads_kernel,
        out_shape=(
            jax.ShapeDtypeStruct(tile, f32),
            jax.ShapeDtypeStruct((2,) + tile, bf16),
            jax.ShapeDtypeStruct(tile, f32),
            jax.ShapeDtypeStruct(probe_modes.shape, bf16),
        ),
        in_specs=[smem] * 2 + [vmem] * 7,
        out_specs=(vmem,) * 4,
        scratch_shapes=[
            pltpu.VMEM((2, layers, parts, 2 * size, size), f32),
            pltpu.VMEM((2, layers, parts, 2 * size, size), f32),
        ],
        compiler_params=pltpu.CompilerParams(vmem_limit_bytes=40 * 1024 * 1024),
    )(counts, corners, own, right, lower, probe_modes, prop, measured, dft)


def body(object_slices, probe_modes, prop_phase, measured, counts, coords):
    tile_rows = object_slices.shape[2]
    tile_cols = object_slices.shape[3]
    col_count = lax.axis_size("col")
    origin = jnp.stack([lax.axis_index("row") * tile_rows, lax.axis_index("col") * tile_cols])
    corners = coords - origin.astype(jnp.int32)
    dft = dft_matrices(probe_modes.shape[-1])
    prop = jnp.stack([jnp.cos(prop_phase), jnp.sin(prop_phase)])
    right = from_behind(object_slices, "col", -1)
    lower = from_behind(jnp.stack([object_slices, right]), "row", -1)
    grad, side, foot, probe_part = local_grads(
        object_slices, right, lower, probe_modes, prop, measured, dft, counts, corners
    )
    side_back = from_behind(side, "col", 1).astype(jnp.float32)
    shares = probe_part.reshape(col_count, -1, probe_part.shape[-1])
    received = lax.all_to_all(shares, "col", 0, 0, tiled=True)
    foot_back = from_behind((foot + side_back[1]).astype(jnp.bfloat16), "row", 1)
    received, foot_back = lax.optimization_barrier((received, foot_back))
    share = jnp.sum(received.astype(jnp.float32), 0).astype(jnp.bfloat16)
    spread = lax.all_to_all(
        jnp.broadcast_to(share[None], shares.shape), "col", 0, 0, tiled=True
    )
    owned = grad + side_back[0] + foot_back.astype(jnp.float32)
    region_slots = measured.shape[0] * col_count
    probe_total = spread.reshape(probe_part.shape).astype(jnp.float32)
    return (owned, (probe_total * (1.0 / math.sqrt(region_slots)))[None])


def solution(mesh):
    return jax.shard_map(
        body,
        mesh=mesh,
        in_specs=(
            P(None, None, "row", "col"),
            P(),
            P(),
            P(("row", "col"), None, None),
            P(("row", "col")),
            P(("row", "col"), None),
        ),
        out_specs=(P(None, None, "row", "col"), P("row", None, None, None, None)),
        check_vma=False,
    )
```

```python
import functools
import math

import jax
import jax.numpy as jnp
from jax import lax
from jax.experimental import pallas as pl
from jax.experimental.pallas import tpu as pltpu
from jax.sharding import PartitionSpec as P


def from_behind(block, axis, distance):
    devices = range(lax.axis_size(axis))
    route = [(i - distance, i) for i in devices if i - distance in devices]
    return lax.ppermute(block, axis, route)


def dft_matrices(size):
    steps_idx = jnp.arange(size, dtype=jnp.int32)
    product_idx = steps_idx[:, None] * steps_idx[None, :] % size
    angle = product_idx.astype(jnp.float32) * (2.0 * math.pi / size)
    scale = 1.0 / math.sqrt(size)
    cos_table = (jnp.cos(angle) * scale).astype(jnp.bfloat16)
    sin_table = (jnp.sin(angle) * scale).astype(jnp.bfloat16)
    minus = jnp.concatenate(
        [
            jnp.concatenate([cos_table, -sin_table], 1),
            jnp.concatenate([sin_table, cos_table], 1),
        ],
        0,
    )
    plus = jnp.concatenate(
        [
            jnp.concatenate([cos_table, sin_table], 1),
            jnp.concatenate([-sin_table, cos_table], 1),
        ],
        0,
    )
    return jnp.stack([minus, plus])


def swap_blocks(matrix, size):
    upper = jnp.concatenate([matrix[:size, :size], matrix[size:, :size]], 1)
    lower = jnp.concatenate([matrix[:size, size:], matrix[size:, size:]], 1)
    return jnp.concatenate([upper, lower], 0)


def transform(waves, first, second):
    size = waves[0][0].shape[0]
    stacked = [
        swap_blocks(jnp.concatenate([real, imag], 0).astype(jnp.bfloat16), size)
        for real, imag in waves
    ]
    halves = first_stage(stacked, first)
    outs = second_stage([swap_blocks(half, size) for half in halves], second)
    return [(out[:size], out[size:]) for out in outs]


def first_stage(stacked, first):
    rows = stacked[0].shape[0]
    half = jnp.dot(
        jnp.concatenate(stacked, 0), first, preferred_element_type=jnp.float32
    ).astype(jnp.bfloat16)
    return [half[i * rows : (i + 1) * rows] for i in range(len(stacked))]


def second_stage(halves, second):
    cols = halves[0].shape[1]
    out = jnp.dot(second, jnp.concatenate(halves, 1), preferred_element_type=jnp.float32)
    return [out[:, i * cols : (i + 1) * cols] for i in range(len(halves))]


def multiply(a_real, a_imag, b_real, b_imag):
    return (a_real * b_real - a_imag * b_imag, a_real * b_imag + a_imag * b_real)


def multiply_conj(a_real, a_imag, b_real, b_imag):
    return (a_real * b_real + a_imag * b_imag, a_imag * b_real - a_real * b_imag)


def grads_kernel(
    counts_ref,
    corner_ref,
    own_ref,
    right_ref,
    lower_ref,
    probe_ref,
    prop_ref,
    measured_ref,
    dft_ref,
    grad_ref,
    side_ref,
    foot_ref,
    probe_out_ref,
    ext_ref,
    acc_ref,
):
    size = probe_ref.shape[-1]
    layers = ext_ref.shape[1]
    pairs = probe_ref.shape[0] // 2
    f32, bf16 = jnp.float32, jnp.bfloat16
    ext_ref[0, :, :, :size] = own_ref[...].astype(f32)
    ext_ref[1, :, :, :size] = right_ref[...].astype(f32)
    ext_ref[0, :, :, size:] = lower_ref[0].astype(f32)
    ext_ref[1, :, :, size:] = lower_ref[1].astype(f32)
    acc_ref[...] = jnp.zeros_like(acc_ref)
    minus, plus = dft_ref[0], dft_ref[1]
    forward = functools.partial(transform, first=minus, second=plus)
    inverse = functools.partial(transform, first=plus, second=minus)

    def twice(block):
        return jnp.concatenate([block, block], 1)

    def fold(block):
        return block[:, :size] + block[:, size:]

    def load_patch(row, col, layer, part):
        rows = pl.ds(row, size)
        both = jnp.concatenate([ext_ref[side, layer, part, rows, :] for side in range(2)], 1)
        return twice(pltpu.roll(both, lax.rem(2 * size - col, 2 * size), 1)[:, :size])

    def visit(count):
        slots = range(count)
        corners = [(corner_ref[slot, 0], corner_ref[slot, 1]) for slot in slots]
        patches = [
            [[load_patch(row, col, layer, part) for part in range(2)] for layer in range(layers)]
            for row, col in corners
        ]
        units = [(which, pair) for which in slots for pair in range(pairs)]
        prop = [twice(prop_ref[part]) for part in range(2)]
        probe = [
            tuple(
                jnp.concatenate([probe_ref[2 * pair, part], probe_ref[2 * pair + 1, part]], 1)
                for part in range(2)
            )
            for pair in range(pairs)
        ]
        entering = [[probe[pair] for _, pair in units]]
        for layer in range(layers):
            leaving = [
                multiply(*wave, *patches[which][layer])
                for wave, (which, _) in zip(entering[layer], units)
            ]
            freqs = forward(leaving)
            if layer < layers - 1:
                entering.append(inverse([multiply(*freq, *prop) for freq in freqs]))
        far = freqs
        residuals = []
        for which, slot in enumerate(slots):
            power = sum(
                real * real + imag * imag
                for (real, imag), unit in zip(far, units)
                if unit[0] == which
            )
            residual = jnp.where(slot < counts_ref[0], fold(power) - measured_ref[slot], 0.0)
            residuals.append(twice(residual))
        back = inverse(
            [
                (residuals[which] * real, residuals[which] * imag)
                for (real, imag), (which, _) in zip(far, units)
            ]
        )
        for layer in reversed(range(layers)):
            terms = [
                multiply_conj(*wave, *entered) for wave, entered in zip(back, entering[layer])
            ]
            for which, (row, col) in enumerate(corners):
                for part in range(2):
                    block = fold(
                        sum(term[part] for term, unit in zip(terms, units) if unit[0] == which)
                    )
                    wide = jnp.concatenate([block, jnp.zeros_like(block)], 1)
                    wide = pltpu.roll(wide, col, 1)
                    rows = pl.ds(row, size)
                    acc_ref[0, layer, part, rows, :] += wide[:, :size]
                    acc_ref[1, layer, part, rows, :] += wide[:, size:]
            to_enter = [
                multiply_conj(*wave, *patches[which][layer])
                for wave, (which, _) in zip(back, units)
            ]
            if layer > 0:
                back = inverse([multiply_conj(*freq, *prop) for freq in forward(to_enter)])
        for pair in range(pairs):
            for part in range(2):
                both = sum(wave[part] for wave, unit in zip(to_enter, units) if unit[1] == pair)
                both = both.astype(bf16)
                probe_out_ref[2 * pair, part] = both[:, :size]
                probe_out_ref[2 * pair + 1, part] = both[:, size:]

    most = measured_ref.shape[0]
    few = (most + 1) // 2
    pl.when(counts_ref[0] <= few)(lambda: visit(few))
    pl.when(counts_ref[0] > few)(lambda: visit(most))
    grad_ref[...] = acc_ref[0, :, :, :size]
    side_ref[...] = acc_ref[1, :, :, :size]
    foot_ref[0] = acc_ref[0, :, :, size:].astype(bf16)
    foot_ref[1] = acc_ref[1, :, :, size:].astype(bf16)


def local_grads(own, right, lower, probe_modes, prop, measured, dft, counts, corners):
    layers, parts, size, _ = own.shape
    f32, bf16 = jnp.float32, jnp.bfloat16
    vmem = pl.BlockSpec(memory_space=pltpu.VMEM)
    smem = pl.BlockSpec(memory_space=pltpu.SMEM)
    tile = (layers, parts, size, size)
    return pl.pallas_call(
        grads_kernel,
        out_shape=(
            jax.ShapeDtypeStruct(tile, f32),
            jax.ShapeDtypeStruct(tile, f32),
            jax.ShapeDtypeStruct((2,) + tile, bf16),
            jax.ShapeDtypeStruct(probe_modes.shape, bf16),
        ),
        in_specs=[smem] * 2 + [vmem] * 7,
        out_specs=(vmem,) * 4,
        scratch_shapes=[
            pltpu.VMEM((2, layers, parts, 2 * size, size), f32),
            pltpu.VMEM((2, layers, parts, 2 * size, size), f32),
        ],
        compiler_params=pltpu.CompilerParams(vmem_limit_bytes=40 * 1024 * 1024),
    )(counts, corners, own, right, lower, probe_modes, prop, measured, dft)


def body(object_slices, probe_modes, prop_phase, measured, counts, coords):
    tile_rows = object_slices.shape[2]
    tile_cols = object_slices.shape[3]
    col_count = lax.axis_size("col")
    origin = jnp.stack([lax.axis_index("row") * tile_rows, lax.axis_index("col") * tile_cols])
    corners = coords - origin.astype(jnp.int32)
    dft = dft_matrices(probe_modes.shape[-1])
    prop = jnp.stack([jnp.cos(prop_phase), jnp.sin(prop_phase)])
    right = from_behind(object_slices, "col", -1)
    lower = from_behind(jnp.stack([object_slices, right]), "row", -1)
    grad, side, foot, probe_part = local_grads(
        object_slices, right, lower, probe_modes, prop, measured, dft, counts, corners
    )
    foot_back = from_behind(foot, "row", 1).astype(jnp.float32)
    shares = probe_part.reshape(col_count, -1, probe_part.shape[-1])
    received = lax.all_to_all(shares, "col", 0, 0, tiled=True)
    side_back = from_behind((side + foot_back[1]).astype(jnp.bfloat16), "col", 1)
    share = jnp.sum(received.astype(jnp.float32), 0).astype(jnp.bfloat16)
    spread = lax.all_to_all(
        jnp.broadcast_to(share[None], shares.shape), "col", 0, 0, tiled=True
    )
    owned = grad + foot_back[0] + side_back.astype(jnp.float32)
    region_slots = measured.shape[0] * col_count
    probe_total = spread.reshape(probe_part.shape).astype(jnp.float32)
    return (owned, (probe_total * (1.0 / math.sqrt(region_slots)))[None])


def solution(mesh):
    return jax.shard_map(
        body,
        mesh=mesh,
        in_specs=(
            P(None, None, "row", "col"),
            P(),
            P(),
            P(("row", "col"), None, None),
            P(("row", "col")),
            P(("row", "col"), None),
        ),
        out_specs=(P(None, None, "row", "col"), P("row", None, None, None, None)),
        check_vma=False,
    )
```

```python
import functools
import math

import jax
import jax.numpy as jnp
from jax import lax
from jax.experimental import pallas as pl
from jax.experimental.pallas import tpu as pltpu
from jax.sharding import PartitionSpec as P


def from_behind(block, axis, distance):
    devices = range(lax.axis_size(axis))
    route = [(i - distance, i) for i in devices if i - distance in devices]
    return lax.ppermute(block, axis, route)


def dft_matrices(size):
    steps_idx = jnp.arange(size, dtype=jnp.int32)
    product_idx = steps_idx[:, None] * steps_idx[None, :] % size
    angle = product_idx.astype(jnp.float32) * (2.0 * math.pi / size)
    scale = 1.0 / math.sqrt(size)
    cos_table = (jnp.cos(angle) * scale).astype(jnp.bfloat16)
    sin_table = (jnp.sin(angle) * scale).astype(jnp.bfloat16)
    minus = jnp.concatenate(
        [
            jnp.concatenate([cos_table, -sin_table], 1),
            jnp.concatenate([sin_table, cos_table], 1),
        ],
        0,
    )
    plus = jnp.concatenate(
        [
            jnp.concatenate([cos_table, sin_table], 1),
            jnp.concatenate([-sin_table, cos_table], 1),
        ],
        0,
    )
    return jnp.stack([minus, plus])


def swap_blocks(matrix, size):
    upper = jnp.concatenate([matrix[:size, :size], matrix[size:, :size]], 1)
    lower = jnp.concatenate([matrix[:size, size:], matrix[size:, size:]], 1)
    return jnp.concatenate([upper, lower], 0)


def transform(waves, first, second):
    size = waves[0][0].shape[0]
    stacked = [
        swap_blocks(jnp.concatenate([real, imag], 0).astype(jnp.bfloat16), size)
        for real, imag in waves
    ]
    halves = first_stage(stacked, first)
    outs = second_stage([swap_blocks(half, size) for half in halves], second)
    return [(out[:size], out[size:]) for out in outs]


def first_stage(stacked, first):
    rows = stacked[0].shape[0]
    half = jnp.dot(
        jnp.concatenate(stacked, 0), first, preferred_element_type=jnp.float32
    ).astype(jnp.bfloat16)
    return [half[i * rows : (i + 1) * rows] for i in range(len(stacked))]


def second_stage(halves, second):
    cols = halves[0].shape[1]
    out = jnp.dot(second, jnp.concatenate(halves, 1), preferred_element_type=jnp.float32)
    return [out[:, i * cols : (i + 1) * cols] for i in range(len(halves))]


def multiply(a_real, a_imag, b_real, b_imag):
    return (a_real * b_real - a_imag * b_imag, a_real * b_imag + a_imag * b_real)


def multiply_conj(a_real, a_imag, b_real, b_imag):
    return (a_real * b_real + a_imag * b_imag, a_imag * b_real - a_real * b_imag)


def grads_kernel(
    counts_ref,
    corner_ref,
    own_ref,
    right_ref,
    lower_ref,
    probe_ref,
    prop_ref,
    measured_ref,
    dft_ref,
    grad_ref,
    side_ref,
    foot_ref,
    probe_out_ref,
    ext_ref,
    acc_ref,
):
    size = probe_ref.shape[-1]
    layers = ext_ref.shape[1]
    pairs = probe_ref.shape[0] // 2
    f32, bf16 = jnp.float32, jnp.bfloat16
    ext_ref[0, :, :, :size] = own_ref[...].astype(f32)
    ext_ref[1, :, :, :size] = right_ref[...].astype(f32)
    ext_ref[0, :, :, size:] = lower_ref[0].astype(f32)
    ext_ref[1, :, :, size:] = lower_ref[1].astype(f32)
    acc_ref[...] = jnp.zeros_like(acc_ref)
    minus, plus = dft_ref[0], dft_ref[1]
    forward = functools.partial(transform, first=minus, second=plus)
    inverse = functools.partial(transform, first=plus, second=minus)

    def twice(block):
        return jnp.concatenate([block, block], 1)

    def fold(block):
        return block[:, :size] + block[:, size:]

    def load_patch(row, col, layer, part):
        rows = pl.ds(row, size)
        both = jnp.concatenate([ext_ref[side, layer, part, rows, :] for side in range(2)], 1)
        return twice(pltpu.roll(both, lax.rem(2 * size - col, 2 * size), 1)[:, :size])

    def visit(count):
        slots = range(count)
        corners = [(corner_ref[slot, 0], corner_ref[slot, 1]) for slot in slots]
        patches = [
            [[load_patch(row, col, layer, part) for part in range(2)] for layer in range(layers)]
            for row, col in corners
        ]
        units = [(which, pair) for which in slots for pair in range(pairs)]
        prop = [twice(prop_ref[part]) for part in range(2)]
        probe = [
            tuple(
                jnp.concatenate([probe_ref[2 * pair, part], probe_ref[2 * pair + 1, part]], 1)
                for part in range(2)
            )
            for pair in range(pairs)
        ]
        entering = [[probe[pair] for _, pair in units]]
        for layer in range(layers):
            leaving = [
                multiply(*wave, *patches[which][layer])
                for wave, (which, _) in zip(entering[layer], units)
            ]
            freqs = forward(leaving)
            if layer < layers - 1:
                entering.append(inverse([multiply(*freq, *prop) for freq in freqs]))
        far = freqs
        residuals = []
        for which, slot in enumerate(slots):
            power = sum(
                real * real + imag * imag
                for (real, imag), unit in zip(far, units)
                if unit[0] == which
            )
            residual = jnp.where(slot < counts_ref[0], fold(power) - measured_ref[slot], 0.0)
            residuals.append(twice(residual))
        back = inverse(
            [
                (residuals[which] * real, residuals[which] * imag)
                for (real, imag), (which, _) in zip(far, units)
            ]
        )
        for layer in reversed(range(layers)):
            terms = [
                multiply_conj(*wave, *entered) for wave, entered in zip(back, entering[layer])
            ]
            for which, (row, col) in enumerate(corners):
                for part in range(2):
                    block = fold(
                        sum(term[part] for term, unit in zip(terms, units) if unit[0] == which)
                    )
                    wide = jnp.concatenate([block, jnp.zeros_like(block)], 1)
                    wide = pltpu.roll(wide, col, 1)
                    rows = pl.ds(row, size)
                    acc_ref[0, layer, part, rows, :] += wide[:, :size]
                    acc_ref[1, layer, part, rows, :] += wide[:, size:]
            to_enter = [
                multiply_conj(*wave, *patches[which][layer])
                for wave, (which, _) in zip(back, units)
            ]
            if layer > 0:
                back = inverse([multiply_conj(*freq, *prop) for freq in forward(to_enter)])
        for pair in range(pairs):
            for part in range(2):
                both = sum(wave[part] for wave, unit in zip(to_enter, units) if unit[1] == pair)
                both = both.astype(bf16)
                probe_out_ref[2 * pair, part] = both[:, :size]
                probe_out_ref[2 * pair + 1, part] = both[:, size:]

    most = measured_ref.shape[0]
    few = (most + 1) // 2
    pl.when(counts_ref[0] <= few)(lambda: visit(few))
    pl.when(counts_ref[0] > few)(lambda: visit(most))
    grad_ref[...] = acc_ref[0, :, :, :size]
    side_ref[...] = acc_ref[1, :, :, :size]
    foot_ref[0] = acc_ref[0, :, :, size:].astype(bf16)
    foot_ref[1] = acc_ref[1, :, :, size:].astype(bf16)


def local_grads(own, right, lower, probe_modes, prop, measured, dft, counts, corners):
    layers, parts, size, _ = own.shape
    f32, bf16 = jnp.float32, jnp.bfloat16
    vmem = pl.BlockSpec(memory_space=pltpu.VMEM)
    smem = pl.BlockSpec(memory_space=pltpu.SMEM)
    tile = (layers, parts, size, size)
    return pl.pallas_call(
        grads_kernel,
        out_shape=(
            jax.ShapeDtypeStruct(tile, f32),
            jax.ShapeDtypeStruct(tile, f32),
            jax.ShapeDtypeStruct((2,) + tile, bf16),
            jax.ShapeDtypeStruct(probe_modes.shape, bf16),
        ),
        in_specs=[smem] * 2 + [vmem] * 7,
        out_specs=(vmem,) * 4,
        scratch_shapes=[
            pltpu.VMEM((2, layers, parts, 2 * size, size), f32),
            pltpu.VMEM((2, layers, parts, 2 * size, size), f32),
        ],
        compiler_params=pltpu.CompilerParams(vmem_limit_bytes=40 * 1024 * 1024),
    )(counts, corners, own, right, lower, probe_modes, prop, measured, dft)


def finish_kernel(grad_ref, foot_ref, side_ref, spread_ref, owned_ref, probe_ref, *, scale):
    f32 = jnp.float32
    owned_ref[...] = grad_ref[...] + foot_ref[0].astype(f32) + side_ref[...].astype(f32)
    probe_ref[...] = spread_ref[...].astype(f32) * scale


def finish(grad, foot_back, side_back, spread, scale):
    vmem = pl.BlockSpec(memory_space=pltpu.VMEM)
    return pl.pallas_call(
        functools.partial(finish_kernel, scale=scale),
        out_shape=(
            jax.ShapeDtypeStruct(grad.shape, jnp.float32),
            jax.ShapeDtypeStruct(spread.shape, jnp.float32),
        ),
        in_specs=[vmem] * 4,
        out_specs=(vmem,) * 2,
        compiler_params=pltpu.CompilerParams(vmem_limit_bytes=16 * 1024 * 1024),
    )(grad, foot_back, side_back, spread)


def body(object_slices, probe_modes, prop_phase, measured, counts, coords):
    tile_rows = object_slices.shape[2]
    tile_cols = object_slices.shape[3]
    col_count = lax.axis_size("col")
    origin = jnp.stack([lax.axis_index("row") * tile_rows, lax.axis_index("col") * tile_cols])
    corners = coords - origin.astype(jnp.int32)
    dft = dft_matrices(probe_modes.shape[-1])
    prop = jnp.stack([jnp.cos(prop_phase), jnp.sin(prop_phase)])
    right = from_behind(object_slices, "col", -1)
    lower = from_behind(jnp.stack([object_slices, right]), "row", -1)
    grad, side, foot, probe_part = local_grads(
        object_slices, right, lower, probe_modes, prop, measured, dft, counts, corners
    )
    foot_back = from_behind(foot, "row", 1)
    shares = probe_part.reshape(col_count, -1, probe_part.shape[-1])
    received = lax.all_to_all(shares, "col", 0, 0, tiled=True)
    side_back = from_behind((side + foot_back[1].astype(jnp.float32)).astype(jnp.bfloat16), "col", 1)
    share = jnp.sum(received.astype(jnp.float32), 0).astype(jnp.bfloat16)
    spread = lax.all_to_all(
        jnp.broadcast_to(share[None], shares.shape), "col", 0, 0, tiled=True
    )
    region_slots = measured.shape[0] * col_count
    owned, probe_total = finish(
        grad, foot_back, side_back, spread, 1.0 / math.sqrt(region_slots)
    )
    return (owned, probe_total.reshape((1,) + probe_part.shape))


def solution(mesh):
    return jax.shard_map(
        body,
        mesh=mesh,
        in_specs=(
            P(None, None, "row", "col"),
            P(),
            P(),
            P(("row", "col"), None, None),
            P(("row", "col")),
            P(("row", "col"), None),
        ),
        out_specs=(P(None, None, "row", "col"), P("row", None, None, None, None)),
        check_vma=False,
    )
```

```python
import functools
import math

import jax
import jax.numpy as jnp
from jax import lax
from jax.experimental import pallas as pl
from jax.experimental.pallas import tpu as pltpu
from jax.sharding import PartitionSpec as P


def from_behind(block, axis, distance):
    devices = range(lax.axis_size(axis))
    route = [(i - distance, i) for i in devices if i - distance in devices]
    return lax.ppermute(block, axis, route)


def from_corner(block, distance):
    rows, cols = lax.axis_size("row"), lax.axis_size("col")
    route = [
        ((i - distance) * cols + j - distance, i * cols + j)
        for i in range(rows)
        for j in range(cols)
        if i - distance in range(rows) and j - distance in range(cols)
    ]
    return lax.ppermute(block, ("row", "col"), route)


def dft_matrices(size):
    steps_idx = jnp.arange(size, dtype=jnp.int32)
    product_idx = steps_idx[:, None] * steps_idx[None, :] % size
    angle = product_idx.astype(jnp.float32) * (2.0 * math.pi / size)
    scale = 1.0 / math.sqrt(size)
    cos_table = (jnp.cos(angle) * scale).astype(jnp.bfloat16)
    sin_table = (jnp.sin(angle) * scale).astype(jnp.bfloat16)
    minus = jnp.concatenate(
        [
            jnp.concatenate([cos_table, -sin_table], 1),
            jnp.concatenate([sin_table, cos_table], 1),
        ],
        0,
    )
    plus = jnp.concatenate(
        [
            jnp.concatenate([cos_table, sin_table], 1),
            jnp.concatenate([-sin_table, cos_table], 1),
        ],
        0,
    )
    return jnp.stack([minus, plus])


def swap_blocks(matrix, size):
    upper = jnp.concatenate([matrix[:size, :size], matrix[size:, :size]], 1)
    lower = jnp.concatenate([matrix[:size, size:], matrix[size:, size:]], 1)
    return jnp.concatenate([upper, lower], 0)


def transform(waves, first, second):
    size = waves[0][0].shape[0]
    stacked = [
        swap_blocks(jnp.concatenate([real, imag], 0).astype(jnp.bfloat16), size)
        for real, imag in waves
    ]
    halves = first_stage(stacked, first)
    outs = second_stage([swap_blocks(half, size) for half in halves], second)
    return [(out[:size], out[size:]) for out in outs]


def first_stage(stacked, first):
    rows = stacked[0].shape[0]
    half = jnp.dot(
        jnp.concatenate(stacked, 0), first, preferred_element_type=jnp.float32
    ).astype(jnp.bfloat16)
    return [half[i * rows : (i + 1) * rows] for i in range(len(stacked))]


def second_stage(halves, second):
    cols = halves[0].shape[1]
    out = jnp.dot(second, jnp.concatenate(halves, 1), preferred_element_type=jnp.float32)
    return [out[:, i * cols : (i + 1) * cols] for i in range(len(halves))]


def multiply(a_real, a_imag, b_real, b_imag):
    return (a_real * b_real - a_imag * b_imag, a_real * b_imag + a_imag * b_real)


def multiply_conj(a_real, a_imag, b_real, b_imag):
    return (a_real * b_real + a_imag * b_imag, a_imag * b_real - a_real * b_imag)


def grads_kernel(
    counts_ref,
    corner_ref,
    own_ref,
    right_ref,
    lower_ref,
    across_ref,
    probe_ref,
    prop_ref,
    measured_ref,
    dft_ref,
    grad_ref,
    side_ref,
    foot_ref,
    probe_out_ref,
    ext_ref,
    acc_ref,
):
    size = probe_ref.shape[-1]
    layers = ext_ref.shape[1]
    pairs = probe_ref.shape[0] // 2
    f32, bf16 = jnp.float32, jnp.bfloat16
    ext_ref[0, :, :, :size] = own_ref[...].astype(f32)
    ext_ref[1, :, :, :size] = right_ref[...].astype(f32)
    ext_ref[0, :, :, size:] = lower_ref[...].astype(f32)
    ext_ref[1, :, :, size:] = across_ref[...].astype(f32)
    acc_ref[...] = jnp.zeros_like(acc_ref)
    minus, plus = dft_ref[0], dft_ref[1]
    forward = functools.partial(transform, first=minus, second=plus)
    inverse = functools.partial(transform, first=plus, second=minus)

    def twice(block):
        return jnp.concatenate([block, block], 1)

    def fold(block):
        return block[:, :size] + block[:, size:]

    def load_patch(row, col, layer, part):
        rows = pl.ds(row, size)
        both = jnp.concatenate([ext_ref[side, layer, part, rows, :] for side in range(2)], 1)
        return twice(pltpu.roll(both, lax.rem(2 * size - col, 2 * size), 1)[:, :size])

    def visit(count):
        slots = range(count)
        corners = [(corner_ref[slot, 0], corner_ref[slot, 1]) for slot in slots]
        patches = [
            [[load_patch(row, col, layer, part) for part in range(2)] for layer in range(layers)]
            for row, col in corners
        ]
        units = [(which, pair) for which in slots for pair in range(pairs)]
        prop = [twice(prop_ref[part]) for part in range(2)]
        probe = [
            tuple(
                jnp.concatenate([probe_ref[2 * pair, part], probe_ref[2 * pair + 1, part]], 1)
                for part in range(2)
            )
            for pair in range(pairs)
        ]
        entering = [[probe[pair] for _, pair in units]]
        for layer in range(layers):
            leaving = [
                multiply(*wave, *patches[which][layer])
                for wave, (which, _) in zip(entering[layer], units)
            ]
            freqs = forward(leaving)
            if layer < layers - 1:
                entering.append(inverse([multiply(*freq, *prop) for freq in freqs]))
        far = freqs
        residuals = []
        for which, slot in enumerate(slots):
            power = sum(
                real * real + imag * imag
                for (real, imag), unit in zip(far, units)
                if unit[0] == which
            )
            residual = jnp.where(slot < counts_ref[0], fold(power) - measured_ref[slot], 0.0)
            residuals.append(twice(residual))
        back = inverse(
            [
                (residuals[which] * real, residuals[which] * imag)
                for (real, imag), (which, _) in zip(far, units)
            ]
        )
        for layer in reversed(range(layers)):
            terms = [
                multiply_conj(*wave, *entered) for wave, entered in zip(back, entering[layer])
            ]
            for which, (row, col) in enumerate(corners):
                for part in range(2):
                    block = fold(
                        sum(term[part] for term, unit in zip(terms, units) if unit[0] == which)
                    )
                    wide = jnp.concatenate([block, jnp.zeros_like(block)], 1)
                    wide = pltpu.roll(wide, col, 1)
                    rows = pl.ds(row, size)
                    acc_ref[0, layer, part, rows, :] += wide[:, :size]
                    acc_ref[1, layer, part, rows, :] += wide[:, size:]
            to_enter = [
                multiply_conj(*wave, *patches[which][layer])
                for wave, (which, _) in zip(back, units)
            ]
            if layer > 0:
                back = inverse([multiply_conj(*freq, *prop) for freq in forward(to_enter)])
        for pair in range(pairs):
            for part in range(2):
                both = sum(wave[part] for wave, unit in zip(to_enter, units) if unit[1] == pair)
                both = both.astype(bf16)
                probe_out_ref[2 * pair, part] = both[:, :size]
                probe_out_ref[2 * pair + 1, part] = both[:, size:]

    most = measured_ref.shape[0]
    few = (most + 1) // 2
    pl.when(counts_ref[0] <= few)(lambda: visit(few))
    pl.when(counts_ref[0] > few)(lambda: visit(most))
    grad_ref[...] = acc_ref[0, :, :, :size]
    side_ref[...] = acc_ref[1, :, :, :size]
    foot_ref[0] = acc_ref[0, :, :, size:].astype(bf16)
    foot_ref[1] = acc_ref[1, :, :, size:].astype(bf16)


def local_grads(own, right, lower, across, probe_modes, prop, measured, dft, counts, corners):
    layers, parts, size, _ = own.shape
    f32, bf16 = jnp.float32, jnp.bfloat16
    vmem = pl.BlockSpec(memory_space=pltpu.VMEM)
    smem = pl.BlockSpec(memory_space=pltpu.SMEM)
    tile = (layers, parts, size, size)
    return pl.pallas_call(
        grads_kernel,
        out_shape=(
            jax.ShapeDtypeStruct(tile, f32),
            jax.ShapeDtypeStruct(tile, f32),
            jax.ShapeDtypeStruct((2,) + tile, bf16),
            jax.ShapeDtypeStruct(probe_modes.shape, bf16),
        ),
        in_specs=[smem] * 2 + [vmem] * 8,
        out_specs=(vmem,) * 4,
        scratch_shapes=[
            pltpu.VMEM((2, layers, parts, 2 * size, size), f32),
            pltpu.VMEM((2, layers, parts, 2 * size, size), f32),
        ],
        compiler_params=pltpu.CompilerParams(vmem_limit_bytes=40 * 1024 * 1024),
    )(counts, corners, own, right, lower, across, probe_modes, prop, measured, dft)


def finish_kernel(grad_ref, foot_ref, side_ref, spread_ref, owned_ref, probe_ref, *, scale):
    f32 = jnp.float32
    owned_ref[...] = grad_ref[...] + foot_ref[0].astype(f32) + side_ref[...].astype(f32)
    probe_ref[...] = spread_ref[...].astype(f32) * scale


def finish(grad, foot_back, side_back, spread, scale):
    vmem = pl.BlockSpec(memory_space=pltpu.VMEM)
    return pl.pallas_call(
        functools.partial(finish_kernel, scale=scale),
        out_shape=(
            jax.ShapeDtypeStruct(grad.shape, jnp.float32),
            jax.ShapeDtypeStruct(spread.shape, jnp.float32),
        ),
        in_specs=[vmem] * 4,
        out_specs=(vmem,) * 2,
        compiler_params=pltpu.CompilerParams(vmem_limit_bytes=16 * 1024 * 1024),
    )(grad, foot_back, side_back, spread)


def body(object_slices, probe_modes, prop_phase, measured, counts, coords):
    tile_rows = object_slices.shape[2]
    tile_cols = object_slices.shape[3]
    col_count = lax.axis_size("col")
    origin = jnp.stack([lax.axis_index("row") * tile_rows, lax.axis_index("col") * tile_cols])
    corners = coords - origin.astype(jnp.int32)
    dft = dft_matrices(probe_modes.shape[-1])
    prop = jnp.stack([jnp.cos(prop_phase), jnp.sin(prop_phase)])
    right = from_behind(object_slices, "col", -1)
    across = from_corner(object_slices, -1)
    lower = from_behind(object_slices, "row", -1)
    grad, side, foot, probe_part = local_grads(
        object_slices, right, lower, across, probe_modes, prop, measured, dft, counts, corners
    )
    foot_back = from_behind(foot, "row", 1)
    shares = probe_part.reshape(col_count, -1, probe_part.shape[-1])
    received = lax.all_to_all(shares, "col", 0, 0, tiled=True)
    side_back = from_behind((side + foot_back[1].astype(jnp.float32)).astype(jnp.bfloat16), "col", 1)
    share = jnp.sum(received.astype(jnp.float32), 0).astype(jnp.bfloat16)
    spread = lax.all_to_all(
        jnp.broadcast_to(share[None], shares.shape), "col", 0, 0, tiled=True
    )
    region_slots = measured.shape[0] * col_count
    owned, probe_total = finish(
        grad, foot_back, side_back, spread, 1.0 / math.sqrt(region_slots)
    )
    return (owned, probe_total.reshape((1,) + probe_part.shape))


def solution(mesh):
    return jax.shard_map(
        body,
        mesh=mesh,
        in_specs=(
            P(None, None, "row", "col"),
            P(),
            P(),
            P(("row", "col"), None, None),
            P(("row", "col")),
            P(("row", "col"), None),
        ),
        out_specs=(P(None, None, "row", "col"), P("row", None, None, None, None)),
        check_vma=False,
    )
```

```python
import functools
import math

import jax
import jax.numpy as jnp
from jax import lax
from jax.experimental import pallas as pl
from jax.experimental.pallas import tpu as pltpu
from jax.sharding import PartitionSpec as P


def from_behind(block, axis, distance):
    devices = range(lax.axis_size(axis))
    route = [(i - distance, i) for i in devices if i - distance in devices]
    return lax.ppermute(block, axis, route)


def from_corner(block, distance):
    rows, cols = lax.axis_size("row"), lax.axis_size("col")
    route = [
        ((i - distance) * cols + j - distance, i * cols + j)
        for i in range(rows)
        for j in range(cols)
        if i - distance in range(rows) and j - distance in range(cols)
    ]
    return lax.ppermute(block, ("row", "col"), route)


def dft_matrices(size):
    steps_idx = jnp.arange(size, dtype=jnp.int32)
    product_idx = steps_idx[:, None] * steps_idx[None, :] % size
    angle = product_idx.astype(jnp.float32) * (2.0 * math.pi / size)
    scale = 1.0 / math.sqrt(size)
    cos_table = (jnp.cos(angle) * scale).astype(jnp.bfloat16)
    sin_table = (jnp.sin(angle) * scale).astype(jnp.bfloat16)
    minus = jnp.concatenate(
        [
            jnp.concatenate([cos_table, -sin_table], 1),
            jnp.concatenate([sin_table, cos_table], 1),
        ],
        0,
    )
    plus = jnp.concatenate(
        [
            jnp.concatenate([cos_table, sin_table], 1),
            jnp.concatenate([-sin_table, cos_table], 1),
        ],
        0,
    )
    return jnp.stack([minus, plus])


def swap_blocks(matrix, size):
    upper = jnp.concatenate([matrix[:size, :size], matrix[size:, :size]], 1)
    lower = jnp.concatenate([matrix[:size, size:], matrix[size:, size:]], 1)
    return jnp.concatenate([upper, lower], 0)


def transform(waves, first, second):
    size = waves[0][0].shape[0]
    stacked = [
        swap_blocks(jnp.concatenate([real, imag], 0).astype(jnp.bfloat16), size)
        for real, imag in waves
    ]
    halves = first_stage(stacked, first)
    outs = second_stage([swap_blocks(half, size) for half in halves], second)
    return [(out[:size], out[size:]) for out in outs]


def first_stage(stacked, first):
    rows = stacked[0].shape[0]
    half = jnp.dot(
        jnp.concatenate(stacked, 0), first, preferred_element_type=jnp.float32
    ).astype(jnp.bfloat16)
    return [half[i * rows : (i + 1) * rows] for i in range(len(stacked))]


def second_stage(halves, second):
    cols = halves[0].shape[1]
    out = jnp.dot(second, jnp.concatenate(halves, 1), preferred_element_type=jnp.float32)
    return [out[:, i * cols : (i + 1) * cols] for i in range(len(halves))]


def multiply(a_real, a_imag, b_real, b_imag):
    return (a_real * b_real - a_imag * b_imag, a_real * b_imag + a_imag * b_real)


def multiply_conj(a_real, a_imag, b_real, b_imag):
    return (a_real * b_real + a_imag * b_imag, a_imag * b_real - a_real * b_imag)


def grads_kernel(
    counts_ref,
    corner_ref,
    own_ref,
    right_ref,
    lower_ref,
    across_ref,
    probe_ref,
    prop_ref,
    measured_ref,
    dft_ref,
    grad_ref,
    side_ref,
    foot_ref,
    probe_out_ref,
    ext_ref,
    acc_ref,
):
    size = probe_ref.shape[-1]
    layers = ext_ref.shape[1]
    pairs = probe_ref.shape[0] // 2
    f32, bf16 = jnp.float32, jnp.bfloat16
    ext_ref[0, :, :, :size] = own_ref[...].astype(f32)
    ext_ref[1, :, :, :size] = right_ref[...].astype(f32)
    ext_ref[0, :, :, size:] = lower_ref[...].astype(f32)
    ext_ref[1, :, :, size:] = across_ref[...].astype(f32)
    acc_ref[...] = jnp.zeros_like(acc_ref)
    minus, plus = dft_ref[0], dft_ref[1]
    forward = functools.partial(transform, first=minus, second=plus)
    inverse = functools.partial(transform, first=plus, second=minus)

    def twice(block):
        return jnp.concatenate([block, block], 1)

    def fold(block):
        return block[:, :size] + block[:, size:]

    def load_patch(row, col, layer, part):
        rows = pl.ds(row, size)
        both = jnp.concatenate([ext_ref[side, layer, part, rows, :] for side in range(2)], 1)
        return twice(pltpu.roll(both, lax.rem(2 * size - col, 2 * size), 1)[:, :size])

    def visit(count):
        slots = range(count)
        corners = [(corner_ref[slot, 0], corner_ref[slot, 1]) for slot in slots]
        patches = [
            [[load_patch(row, col, layer, part) for part in range(2)] for layer in range(layers)]
            for row, col in corners
        ]
        units = [(which, pair) for which in slots for pair in range(pairs)]
        prop = [twice(prop_ref[part]) for part in range(2)]
        probe = [
            tuple(
                jnp.concatenate([probe_ref[2 * pair, part], probe_ref[2 * pair + 1, part]], 1)
                for part in range(2)
            )
            for pair in range(pairs)
        ]
        entering = [[probe[pair] for _, pair in units]]
        for layer in range(layers):
            leaving = [
                multiply(*wave, *patches[which][layer])
                for wave, (which, _) in zip(entering[layer], units)
            ]
            freqs = forward(leaving)
            if layer < layers - 1:
                entering.append(inverse([multiply(*freq, *prop) for freq in freqs]))
        far = freqs
        residuals = []
        for which, slot in enumerate(slots):
            power = sum(
                real * real + imag * imag
                for (real, imag), unit in zip(far, units)
                if unit[0] == which
            )
            residual = jnp.where(slot < counts_ref[0], fold(power) - measured_ref[slot], 0.0)
            residuals.append(twice(residual))
        back = inverse(
            [
                (residuals[which] * real, residuals[which] * imag)
                for (real, imag), (which, _) in zip(far, units)
            ]
        )
        for layer in reversed(range(layers)):
            terms = [
                multiply_conj(*wave, *entered) for wave, entered in zip(back, entering[layer])
            ]
            for which, (row, col) in enumerate(corners):
                for part in range(2):
                    block = fold(
                        sum(term[part] for term, unit in zip(terms, units) if unit[0] == which)
                    )
                    wide = jnp.concatenate([block, jnp.zeros_like(block)], 1)
                    wide = pltpu.roll(wide, col, 1)
                    rows = pl.ds(row, size)
                    acc_ref[0, layer, part, rows, :] += wide[:, :size]
                    acc_ref[1, layer, part, rows, :] += wide[:, size:]
            to_enter = [
                multiply_conj(*wave, *patches[which][layer])
                for wave, (which, _) in zip(back, units)
            ]
            if layer > 0:
                back = inverse([multiply_conj(*freq, *prop) for freq in forward(to_enter)])
        for pair in range(pairs):
            for part in range(2):
                both = sum(wave[part] for wave, unit in zip(to_enter, units) if unit[1] == pair)
                both = both.astype(bf16)
                probe_out_ref[2 * pair, part] = both[:, :size]
                probe_out_ref[2 * pair + 1, part] = both[:, size:]

    most = measured_ref.shape[0]
    few = (most + 1) // 2
    live = counts_ref[0]
    pl.when(live <= 1)(lambda: visit(1))
    pl.when((live > 1) & (live <= few))(lambda: visit(few))
    pl.when(live > few)(lambda: visit(most))
    grad_ref[...] = acc_ref[0, :, :, :size]
    side_ref[...] = acc_ref[1, :, :, :size]
    foot_ref[0] = acc_ref[0, :, :, size:].astype(bf16)
    foot_ref[1] = acc_ref[1, :, :, size:].astype(bf16)


def local_grads(own, right, lower, across, probe_modes, prop, measured, dft, counts, corners):
    layers, parts, size, _ = own.shape
    f32, bf16 = jnp.float32, jnp.bfloat16
    vmem = pl.BlockSpec(memory_space=pltpu.VMEM)
    smem = pl.BlockSpec(memory_space=pltpu.SMEM)
    tile = (layers, parts, size, size)
    return pl.pallas_call(
        grads_kernel,
        out_shape=(
            jax.ShapeDtypeStruct(tile, f32),
            jax.ShapeDtypeStruct(tile, f32),
            jax.ShapeDtypeStruct((2,) + tile, bf16),
            jax.ShapeDtypeStruct(probe_modes.shape, bf16),
        ),
        in_specs=[smem] * 2 + [vmem] * 8,
        out_specs=(vmem,) * 4,
        scratch_shapes=[
            pltpu.VMEM((2, layers, parts, 2 * size, size), f32),
            pltpu.VMEM((2, layers, parts, 2 * size, size), f32),
        ],
        compiler_params=pltpu.CompilerParams(vmem_limit_bytes=40 * 1024 * 1024),
    )(counts, corners, own, right, lower, across, probe_modes, prop, measured, dft)


def finish_kernel(grad_ref, foot_ref, side_ref, spread_ref, owned_ref, probe_ref, *, scale):
    f32 = jnp.float32
    owned_ref[...] = grad_ref[...] + foot_ref[0].astype(f32) + side_ref[...].astype(f32)
    probe_ref[...] = spread_ref[...].astype(f32) * scale


def finish(grad, foot_back, side_back, spread, scale):
    vmem = pl.BlockSpec(memory_space=pltpu.VMEM)
    return pl.pallas_call(
        functools.partial(finish_kernel, scale=scale),
        out_shape=(
            jax.ShapeDtypeStruct(grad.shape, jnp.float32),
            jax.ShapeDtypeStruct(spread.shape, jnp.float32),
        ),
        in_specs=[vmem] * 4,
        out_specs=(vmem,) * 2,
        compiler_params=pltpu.CompilerParams(vmem_limit_bytes=16 * 1024 * 1024),
    )(grad, foot_back, side_back, spread)


def body(object_slices, probe_modes, prop_phase, measured, counts, coords):
    tile_rows = object_slices.shape[2]
    tile_cols = object_slices.shape[3]
    col_count = lax.axis_size("col")
    origin = jnp.stack([lax.axis_index("row") * tile_rows, lax.axis_index("col") * tile_cols])
    corners = coords - origin.astype(jnp.int32)
    dft = dft_matrices(probe_modes.shape[-1])
    prop = jnp.stack([jnp.cos(prop_phase), jnp.sin(prop_phase)])
    right = from_behind(object_slices, "col", -1)
    across = from_corner(object_slices, -1)
    lower = from_behind(object_slices, "row", -1)
    grad, side, foot, probe_part = local_grads(
        object_slices, right, lower, across, probe_modes, prop, measured, dft, counts, corners
    )
    foot_back = from_behind(foot, "row", 1)
    shares = probe_part.reshape(col_count, -1, probe_part.shape[-1])
    received = lax.all_to_all(shares, "col", 0, 0, tiled=True)
    side_back = from_behind((side + foot_back[1].astype(jnp.float32)).astype(jnp.bfloat16), "col", 1)
    share = jnp.sum(received.astype(jnp.float32), 0).astype(jnp.bfloat16)
    spread = lax.all_to_all(
        jnp.broadcast_to(share[None], shares.shape), "col", 0, 0, tiled=True
    )
    region_slots = measured.shape[0] * col_count
    owned, probe_total = finish(
        grad, foot_back, side_back, spread, 1.0 / math.sqrt(region_slots)
    )
    return (owned, probe_total.reshape((1,) + probe_part.shape))


def solution(mesh):
    return jax.shard_map(
        body,
        mesh=mesh,
        in_specs=(
            P(None, None, "row", "col"),
            P(),
            P(),
            P(("row", "col"), None, None),
            P(("row", "col")),
            P(("row", "col"), None),
        ),
        out_specs=(P(None, None, "row", "col"), P("row", None, None, None, None)),
        check_vma=False,
    )
```

```python
import functools
import math

import jax
import jax.numpy as jnp
from jax import lax
from jax.experimental import pallas as pl
from jax.experimental.pallas import tpu as pltpu
from jax.sharding import PartitionSpec as P


def from_behind(block, axis, distance):
    devices = range(lax.axis_size(axis))
    route = [(i - distance, i) for i in devices if i - distance in devices]
    return lax.ppermute(block, axis, route)


def from_corner(block, distance):
    rows, cols = lax.axis_size("row"), lax.axis_size("col")
    route = [
        ((i - distance) * cols + j - distance, i * cols + j)
        for i in range(rows)
        for j in range(cols)
        if i - distance in range(rows) and j - distance in range(cols)
    ]
    return lax.ppermute(block, ("row", "col"), route)


def dft_matrices(size):
    steps_idx = jnp.arange(size, dtype=jnp.int32)
    product_idx = steps_idx[:, None] * steps_idx[None, :] % size
    angle = product_idx.astype(jnp.float32) * (2.0 * math.pi / size)
    scale = 1.0 / math.sqrt(size)
    cos_table = (jnp.cos(angle) * scale).astype(jnp.bfloat16)
    sin_table = (jnp.sin(angle) * scale).astype(jnp.bfloat16)
    minus = jnp.concatenate(
        [
            jnp.concatenate([cos_table, -sin_table], 1),
            jnp.concatenate([sin_table, cos_table], 1),
        ],
        0,
    )
    plus = jnp.concatenate(
        [
            jnp.concatenate([cos_table, sin_table], 1),
            jnp.concatenate([-sin_table, cos_table], 1),
        ],
        0,
    )
    return jnp.stack([minus, plus])


def swap_blocks(matrix, size):
    upper = jnp.concatenate([matrix[:size, :size], matrix[size:, :size]], 1)
    lower = jnp.concatenate([matrix[:size, size:], matrix[size:, size:]], 1)
    return jnp.concatenate([upper, lower], 0)


def transform(waves, first, second):
    size = waves[0][0].shape[0]
    stacked = [
        swap_blocks(jnp.concatenate([real, imag], 0).astype(jnp.bfloat16), size)
        for real, imag in waves
    ]
    halves = first_stage(stacked, first)
    outs = second_stage([swap_blocks(half, size) for half in halves], second)
    return [(out[:size], out[size:]) for out in outs]


def first_stage(stacked, first):
    rows = stacked[0].shape[0]
    half = jnp.dot(
        jnp.concatenate(stacked, 0), first, preferred_element_type=jnp.float32
    ).astype(jnp.bfloat16)
    return [half[i * rows : (i + 1) * rows] for i in range(len(stacked))]


def second_stage(halves, second):
    cols = halves[0].shape[1]
    out = jnp.dot(second, jnp.concatenate(halves, 1), preferred_element_type=jnp.float32)
    return [out[:, i * cols : (i + 1) * cols] for i in range(len(halves))]


def multiply(a_real, a_imag, b_real, b_imag):
    return (a_real * b_real - a_imag * b_imag, a_real * b_imag + a_imag * b_real)


def multiply_conj(a_real, a_imag, b_real, b_imag):
    return (a_real * b_real + a_imag * b_imag, a_imag * b_real - a_real * b_imag)


def grads_kernel(
    counts_ref,
    corner_ref,
    own_ref,
    right_ref,
    lower_ref,
    across_ref,
    probe_ref,
    prop_ref,
    measured_ref,
    dft_ref,
    grad_ref,
    side_ref,
    foot_ref,
    probe_out_ref,
    ext_ref,
    acc_ref,
):
    size = probe_ref.shape[-1]
    layers = ext_ref.shape[1]
    pairs = probe_ref.shape[0] // 2
    f32, bf16 = jnp.float32, jnp.bfloat16
    ext_ref[0, :, :, :size] = own_ref[...].astype(f32)
    ext_ref[1, :, :, :size] = right_ref[...].astype(f32)
    ext_ref[0, :, :, size:] = lower_ref[...].astype(f32)
    ext_ref[1, :, :, size:] = across_ref[...].astype(f32)
    acc_ref[...] = jnp.zeros_like(acc_ref)
    minus, plus = dft_ref[0], dft_ref[1]
    forward = functools.partial(transform, first=minus, second=plus)
    inverse = functools.partial(transform, first=plus, second=minus)

    def twice(block):
        return jnp.concatenate([block, block], 1)

    def fold(block):
        return block[:, :size] + block[:, size:]

    def load_patch(row, col, layer, part):
        rows = pl.ds(row, size)
        both = jnp.concatenate([ext_ref[side, layer, part, rows, :] for side in range(2)], 1)
        return twice(pltpu.roll(both, lax.rem(2 * size - col, 2 * size), 1)[:, :size])

    def visit(count):
        slots = range(count)
        corners = [(corner_ref[slot, 0], corner_ref[slot, 1]) for slot in slots]
        patches = [
            [[load_patch(row, col, layer, part) for part in range(2)] for layer in range(layers)]
            for row, col in corners
        ]
        units = [(which, pair) for which in slots for pair in range(pairs)]
        prop = [twice(prop_ref[part]) for part in range(2)]
        probe = [
            tuple(
                jnp.concatenate([probe_ref[2 * pair, part], probe_ref[2 * pair + 1, part]], 1)
                for part in range(2)
            )
            for pair in range(pairs)
        ]
        entering = [[probe[pair] for _, pair in units]]
        for layer in range(layers):
            leaving = [
                multiply(*wave, *patches[which][layer])
                for wave, (which, _) in zip(entering[layer], units)
            ]
            freqs = forward(leaving)
            if layer < layers - 1:
                entering.append(inverse([multiply(*freq, *prop) for freq in freqs]))
        far = freqs
        residuals = []
        for which, slot in enumerate(slots):
            power = sum(
                real * real + imag * imag
                for (real, imag), unit in zip(far, units)
                if unit[0] == which
            )
            residual = jnp.where(slot < counts_ref[0], fold(power) - measured_ref[slot], 0.0)
            residuals.append(twice(residual))
        back = inverse(
            [
                (residuals[which] * real, residuals[which] * imag)
                for (real, imag), (which, _) in zip(far, units)
            ]
        )
        for layer in reversed(range(layers)):
            terms = [
                multiply_conj(*wave, *entered) for wave, entered in zip(back, entering[layer])
            ]
            for which, (row, col) in enumerate(corners):
                for part in range(2):
                    block = fold(
                        sum(term[part] for term, unit in zip(terms, units) if unit[0] == which)
                    )
                    wide = jnp.concatenate([block, jnp.zeros_like(block)], 1)
                    wide = pltpu.roll(wide, col, 1)
                    rows = pl.ds(row, size)
                    acc_ref[0, layer, part, rows, :] += wide[:, :size]
                    acc_ref[1, layer, part, rows, :] += wide[:, size:]
            to_enter = [
                multiply_conj(*wave, *patches[which][layer])
                for wave, (which, _) in zip(back, units)
            ]
            if layer > 0:
                back = inverse([multiply_conj(*freq, *prop) for freq in forward(to_enter)])
        for pair in range(pairs):
            for part in range(2):
                both = sum(wave[part] for wave, unit in zip(to_enter, units) if unit[1] == pair)
                both = both.astype(bf16)
                probe_out_ref[2 * pair, part] = both[:, :size]
                probe_out_ref[2 * pair + 1, part] = both[:, size:]

    most = measured_ref.shape[0]
    few = (most + 1) // 2
    pl.when(counts_ref[0] <= few)(lambda: visit(few))
    pl.when(counts_ref[0] > few)(lambda: visit(most))
    grad_ref[...] = acc_ref[0, :, :, :size]
    side_ref[...] = acc_ref[1, :, :, :size]
    foot_ref[0] = acc_ref[0, :, :, size:].astype(bf16)
    foot_ref[1] = acc_ref[1, :, :, size:].astype(bf16)


def local_grads(own, right, lower, across, probe_modes, prop, measured, dft, counts, corners):
    layers, parts, size, _ = own.shape
    f32, bf16 = jnp.float32, jnp.bfloat16
    vmem = pl.BlockSpec(memory_space=pltpu.VMEM)
    smem = pl.BlockSpec(memory_space=pltpu.SMEM)
    tile = (layers, parts, size, size)
    return pl.pallas_call(
        grads_kernel,
        out_shape=(
            jax.ShapeDtypeStruct(tile, f32),
            jax.ShapeDtypeStruct(tile, f32),
            jax.ShapeDtypeStruct((2,) + tile, bf16),
            jax.ShapeDtypeStruct(probe_modes.shape, bf16),
        ),
        in_specs=[smem] * 2 + [vmem] * 8,
        out_specs=(vmem,) * 4,
        scratch_shapes=[
            pltpu.VMEM((2, layers, parts, 2 * size, size), f32),
            pltpu.VMEM((2, layers, parts, 2 * size, size), f32),
        ],
        compiler_params=pltpu.CompilerParams(vmem_limit_bytes=40 * 1024 * 1024),
    )(counts, corners, own, right, lower, across, probe_modes, prop, measured, dft)


def finish_kernel(grad_ref, foot_ref, side_ref, spread_ref, owned_ref, probe_ref, *, scale):
    f32 = jnp.float32
    owned_ref[...] = grad_ref[...] + foot_ref[0].astype(f32) + side_ref[...].astype(f32)
    probe_ref[...] = spread_ref[...].astype(f32) * scale


def finish(grad, foot_back, side_back, spread, scale):
    vmem = pl.BlockSpec(memory_space=pltpu.VMEM)
    return pl.pallas_call(
        functools.partial(finish_kernel, scale=scale),
        out_shape=(
            jax.ShapeDtypeStruct(grad.shape, jnp.float32),
            jax.ShapeDtypeStruct(spread.shape, jnp.float32),
        ),
        in_specs=[vmem] * 4,
        out_specs=(vmem,) * 2,
        compiler_params=pltpu.CompilerParams(vmem_limit_bytes=16 * 1024 * 1024),
    )(grad, foot_back, side_back, spread)


def body(object_slices, probe_modes, prop_phase, measured, counts, coords):
    tile_rows = object_slices.shape[2]
    tile_cols = object_slices.shape[3]
    col_count = lax.axis_size("col")
    origin = jnp.stack([lax.axis_index("row") * tile_rows, lax.axis_index("col") * tile_cols])
    corners = coords - origin.astype(jnp.int32)
    dft = dft_matrices(probe_modes.shape[-1])
    prop = jnp.stack([jnp.cos(prop_phase), jnp.sin(prop_phase)])
    across = from_corner(object_slices, -1)
    right = from_behind(object_slices, "col", -1)
    lower = from_behind(object_slices, "row", -1)
    grad, side, foot, probe_part = local_grads(
        object_slices, right, lower, across, probe_modes, prop, measured, dft, counts, corners
    )
    foot_back = from_behind(foot, "row", 1)
    shares = probe_part.reshape(col_count, -1, probe_part.shape[-1])
    received = lax.all_to_all(shares, "col", 0, 0, tiled=True)
    side_back = from_behind((side + foot_back[1].astype(jnp.float32)).astype(jnp.bfloat16), "col", 1)
    share = jnp.sum(received.astype(jnp.float32), 0).astype(jnp.bfloat16)
    spread = lax.all_to_all(
        jnp.broadcast_to(share[None], shares.shape), "col", 0, 0, tiled=True
    )
    region_slots = measured.shape[0] * col_count
    owned, probe_total = finish(
        grad, foot_back, side_back, spread, 1.0 / math.sqrt(region_slots)
    )
    return (owned, probe_total.reshape((1,) + probe_part.shape))


def solution(mesh):
    return jax.shard_map(
        body,
        mesh=mesh,
        in_specs=(
            P(None, None, "row", "col"),
            P(),
            P(),
            P(("row", "col"), None, None),
            P(("row", "col")),
            P(("row", "col"), None),
        ),
        out_specs=(P(None, None, "row", "col"), P("row", None, None, None, None)),
        check_vma=False,
    )
```
